256 devices in a mesh: section: 4 (over x), pack: 32 (over z, y), tensor: 2 (over core).
Axes of the slice: x: 4, y: 4, z: 8, core: 2. Of those that a mesh axis runs over, the one named last changes fastest.
Arguments:
- queries: bfloat16 [4, 16384, 2560], P('section', 'pack', 'tensor')
- keys: bfloat16 [4, 16384, 2560], P('section', 'pack', 'tensor')
- values: bfloat16 [4, 16384, 2560], P('section', 'pack', 'tensor'), may hold values from -6 to 6
- seg_len: int32 [4, 32, 16], replicated, may hold values from 1 to 64, as said below
Outputs:
- context: bfloat16 [4, 16384, 2560], P('section', ('pack', 'tensor'))
The draws below stay inside these ranges and needn't reach their ends.
Inputs may be any that keep to these rules, and one draw needn't show every extreme that they name: seg_len[m, p] lists in order the lengths of the 16 segments of home p's rows; they sum to 512, and each home has a segment of exactly 64 rows.
All inputs are finite; a program needn't handle non-finite values.
Results may differ from the reference program's by a relative error of at most 0.0049.
Values may be sent and summed in bfloat16 or wider, within the bound.
A program may use at most 128 MiB of HBM per device.

```python
import math
import jax
import jax.numpy as jnp
from jax import lax

HEADS = 20
HEAD_DIM = 128
MICRO = 4
HOMES = 32
SEGS = 16
CAPACITY = 64
TOKENS = 16384


def shared_rows(key):
    return jax.random.normal(key, (MICRO, TOKENS, HEADS * HEAD_DIM), jnp.float32)


def draw_keys(key, part):
    shared = shared_rows(key)
    return shared.astype(jnp.bfloat16)


def draw_queries(key, part):
    key = jax.random.fold_in(key, 13)
    full_shape = (MICRO, TOKENS, HEADS * HEAD_DIM)
    return jax.random.normal(key, full_shape, jnp.float32).astype(jnp.bfloat16)


def draw_seg_len(key, part):
    key = jax.random.fold_in(key, 3)
    half_cap = CAPACITY // 2
    pair_count = (SEGS - 4) // 2

    def one_home(subkey):
        key_amp, key_sign, key_lead, key_order = jax.random.split(subkey, 4)
        amplitude = jax.random.randint(key_amp, (pair_count,), 0, half_cap)
        signed = (jax.random.randint(key_sign, (pair_count,), 0, 2) * 2 - 1) * amplitude
        leading = jax.random.randint(key_lead, (2,), 1, half_cap)
        anchors = jnp.stack([jnp.int32(CAPACITY), leading[0], leading[1], CAPACITY - leading[0] - leading[1]])
        lengths = jnp.concatenate([anchors, half_cap + signed, half_cap - signed]).astype(jnp.int32)
        return lengths[jax.random.permutation(key_order, SEGS)]
    subkeys = jax.random.split(key, MICRO * HOMES)
    return jax.vmap(one_home)(subkeys).reshape(MICRO, HOMES, SEGS)


def levels(stream_key, dims, shards, low, high):
    gain = 1.0
    for position, parts in shards:
        steps = jax.random.uniform(jax.random.fold_in(jax.random.fold_in(stream_key, 6), position), (parts,), jnp.float32, low / len(shards), high / len(shards))
        gain = gain * jnp.repeat(jnp.exp(steps), dims[position] // parts).reshape((-1,) + (1,) * (len(dims) - 1 - position))
    return gain


def centred(own_key, dims, scale, most, cuts=(), kind=jnp.bfloat16):
    entries = jax.random.normal(own_key, dims, jnp.float32) * scale
    if len(cuts) > 0:
        entries = levels(own_key, dims, cuts, -0.22, 0.18) * entries
    return jnp.clip(entries, min=-most, max=most).astype(kind)


def setup_inputs(seed: int = 0) -> dict:
    seeds = jax.random.split(jax.random.key(seed), 5)
    queries = draw_queries(jax.random.fold_in(seeds[4], 71), 0)
    keys = draw_keys(jax.random.fold_in(seeds[4], 71), 0)
    values = centred(seeds[2], (MICRO, TOKENS, HEADS * HEAD_DIM), 1.0, 6.0, ((0, 4), (1, 32), (2, 2)))
    seg_len = draw_seg_len(jax.random.fold_in(seeds[4], 71), 0)
    return {"queries": queries, "keys": keys, "values": values, "seg_len": seg_len}


masked_score = -1e+30

def row_labels(lengths):
    seg_ids = jnp.arange(HOMES * SEGS, dtype=jnp.int32).reshape(HOMES, SEGS)
    joined = jnp.concatenate([seg_ids[:1, 0], seg_ids[:-1, SEGS - 1]])
    seg_ids = seg_ids.at[:, 0].set(joined)
    return jnp.repeat(seg_ids.reshape(-1), lengths.reshape(-1), total_repeat_length=TOKENS).astype(jnp.int32)

def attend_micro(query_rows, key_rows, value_rows, lengths):
    labels = row_labels(lengths)
    margin = 2 * CAPACITY
    block_rows = 2 * CAPACITY
    full_shape = (TOKENS, HEADS, HEAD_DIM)
    query_rows = query_rows.reshape(full_shape)
    padding = jnp.zeros((margin, HEADS, HEAD_DIM), key_rows.dtype)
    key_pad = jnp.concatenate([padding, key_rows.reshape(full_shape), padding])
    value_pad = jnp.concatenate([padding, value_rows.reshape(full_shape), padding])
    outside = jnp.full((margin,), -1, jnp.int32)
    label_pad = jnp.concatenate([outside, labels, outside])
    score_scale = 1.0 / math.sqrt(HEAD_DIM)

    def one_block(block_index):
        start = block_index * block_rows
        query_block = lax.dynamic_slice_in_dim(query_rows, start, block_rows, 0).astype(jnp.float32)
        key_block = lax.dynamic_slice_in_dim(key_pad, start, block_rows + 2 * margin, 0).astype(jnp.float32)
        value_block = lax.dynamic_slice_in_dim(value_pad, start, block_rows + 2 * margin, 0).astype(jnp.float32)
        label_query = lax.dynamic_slice_in_dim(labels, start, block_rows, 0)
        label_key = lax.dynamic_slice_in_dim(label_pad, start, block_rows + 2 * margin, 0)
        scores = jnp.einsum('qhd,khd->hqk', query_block, key_block) * score_scale
        scores = jnp.where((label_query[:, None] == label_key[None, :])[None], scores, masked_score)
        row_max = lax.optimization_barrier(jnp.max(scores, axis=2, keepdims=True))
        weights = jnp.exp(scores - row_max)
        weights = (weights / lax.optimization_barrier(jnp.sum(weights, axis=2, keepdims=True))).astype(jnp.bfloat16)
        mixed = jnp.einsum('hqk,khd->qhd', weights.astype(jnp.float32), value_block)
        return mixed.astype(jnp.bfloat16)
    blocks = lax.map(one_block, jnp.arange(TOKENS // block_rows, dtype=jnp.int32))
    return blocks.reshape(TOKENS, HEADS * HEAD_DIM)

def reference(queries, keys, values, seg_len):
    attended = jnp.stack([attend_micro(queries[micro], keys[micro], values[micro], seg_len[micro]) for micro in range(MICRO)])
    return jnp.roll(attended, 1, axis=0)
```

```python
import functools
import math

import jax
import jax.numpy as jnp
from jax import lax
from jax.experimental import pallas as pl
from jax.experimental.pallas import tpu as pltpu
from jax.sharding import PartitionSpec as P

HEAD_DIM = 128
HALO = 64
BLOCK = 128
WINDOW = BLOCK + 2 * HALO
MESH = pl.DeviceIdType.MESH
MASKED = -3.0e38


def kernel(
    sizes,
    len_ref,
    q_hbm,
    k_hbm,
    v_hbm,
    out_ref,
    q_buf,
    k_buf,
    v_buf,
    bias,
    stage,
    relay_one,
    relay_two,
    load_sem,
    halo_send,
    halo_recv,
    out_send,
    out_recv,
    one_recv,
    one_send,
    two_recv,
    two_send,
):
    sections, homes, heads, rows, segs = sizes
    feats = heads * HEAD_DIM
    s, p, t = lax.axis_index("section"), lax.axis_index("pack"), lax.axis_index("tensor")
    ahead, behind = lax.rem(s + 1, sections), lax.rem(s + sections - 1, sections)
    after, before = lax.rem(p + 1, homes), lax.rem(p + homes - 1, homes)

    barrier = pltpu.get_barrier_semaphore()
    partners = [
        (ahead, p, t),
        (ahead, p, 1 - t),
        (behind, p, t),
        (behind, p, 1 - t),
        (s, after, t),
        (s, before, t),
    ]
    for partner in partners:
        pl.semaphore_signal(barrier, inc=1, device_id=partner, device_id_type=MESH)

    own = pl.ds(HALO, rows)
    loads = [
        pltpu.make_async_copy(q_hbm.at[0], q_buf, load_sem.at[0]),
        pltpu.make_async_copy(k_hbm.at[0], k_buf.at[own], load_sem.at[1]),
        pltpu.make_async_copy(v_hbm.at[0], v_buf.at[own], load_sem.at[2]),
    ]
    for load in loads:
        load.start()

    thresholds = [jnp.where(p > 0, -len_ref[s, segs - 1, before], 0)]
    end = jnp.int32(0)
    for j in range(segs - 1):
        end = end + len_ref[s, j, p]
        thresholds.append(end)
    thresholds.append(rows + jnp.where(p < homes - 1, len_ref[s, 0, after], 0))

    def labels(position):
        total = jnp.zeros(position.shape, jnp.int32)
        for threshold in thresholds:
            total = total + jnp.where(position >= threshold, 1, 0)
        return total

    key_label = labels(lax.broadcasted_iota(jnp.int32, (8, rows + 2 * HALO), 1) - HALO)
    for b in range(rows // BLOCK):
        query_label = labels(lax.broadcasted_iota(jnp.int32, (BLOCK, 128), 0) + b * BLOCK)
        for c in range(WINDOW // 128):
            start = b * BLOCK + c * 128
            same = query_label == key_label[0:1, start : start + 128]
            bias[b, :, c * 128 : c * 128 + 128] = jnp.where(same, 0.0, MASKED)

    pl.semaphore_wait(barrier, len(partners))

    def head_cols(h):
        return pl.ds(pl.multiple_of(h * HEAD_DIM, HEAD_DIM), HEAD_DIM)

    def halo_copies(h):
        cols = head_cols(h)
        copies = []
        for n, (source, buf) in enumerate(((k_hbm, k_buf), (v_hbm, v_buf))):
            copies.append(
                pltpu.make_async_remote_copy(
                    src_ref=source.at[0, pl.ds(rows - HALO, HALO), cols],
                    dst_ref=buf.at[pl.ds(0, HALO), cols],
                    send_sem=halo_send.at[n, h],
                    recv_sem=halo_recv.at[n, h],
                    device_id=(s, after, t),
                    device_id_type=MESH,
                )
            )
            copies.append(
                pltpu.make_async_remote_copy(
                    src_ref=source.at[0, pl.ds(0, HALO), cols],
                    dst_ref=buf.at[pl.ds(HALO + rows, HALO), cols],
                    send_sem=halo_send.at[n + 2, h],
                    recv_sem=halo_recv.at[n + 2, h],
                    device_id=(s, before, t),
                    device_id_type=MESH,
                )
            )
        return copies

    def start_halo(h, carry):
        for copy in halo_copies(h):
            copy.start()
        return carry

    lax.fori_loop(0, heads, start_halo, 0)

    for load in loads:
        load.wait()

    factor = math.log2(math.e) / math.sqrt(HEAD_DIM)

    def attend(b, h):
        cols = head_cols(h)
        scores = lax.dot_general(
            q_buf[b * BLOCK : (b + 1) * BLOCK, cols],
            k_buf[b * BLOCK : b * BLOCK + WINDOW, cols],
            (((1,), (1,)), ((), ())),
            preferred_element_type=jnp.float32,
        )
        scores = scores + bias[b]
        row_max = jnp.max(scores, axis=1, keepdims=True)
        weights = jnp.exp2((scores - row_max) * factor)
        weights = weights * (1.0 / jnp.sum(weights, axis=1, keepdims=True))
        mixed = jnp.dot(
            weights.astype(jnp.bfloat16),
            v_buf[b * BLOCK : b * BLOCK + WINDOW, cols],
            preferred_element_type=jnp.float32,
        )
        stage[b, h] = mixed.astype(jnp.bfloat16)

    def final_place(b, h):
        start = pl.multiple_of(t * feats + h * HEAD_DIM, HEAD_DIM)
        return out_ref.at[pl.ds((b % 2) * BLOCK, BLOCK), pl.ds(start, HEAD_DIM)]

    def forward(b, h):
        return pltpu.make_async_remote_copy(
            src_ref=stage.at[b, h],
            dst_ref=final_place(b, h),
            send_sem=out_send,
            recv_sem=out_recv,
            device_id=(ahead, p, b // 2),
            device_id_type=MESH,
        )

    def hop_one(h):
        return pltpu.make_async_remote_copy(
            src_ref=stage.at[1, h],
            dst_ref=relay_one.at[h],
            send_sem=out_send,
            recv_sem=one_recv.at[h],
            device_id=(behind, p, t),
            device_id_type=MESH,
        )

    def hop_two(h):
        return pltpu.make_async_remote_copy(
            src_ref=relay_one.at[h],
            dst_ref=relay_two.at[h],
            send_sem=one_send,
            recv_sem=two_recv.at[h],
            device_id=(behind, p, t),
            device_id_type=MESH,
        )

    def hop_three(h):
        return pltpu.make_async_remote_copy(
            src_ref=relay_two.at[h],
            dst_ref=final_place(1, h),
            send_sem=two_send,
            recv_sem=out_recv,
            device_id=(behind, p, 0),
            device_id_type=MESH,
        )

    def inner(h, carry):
        attend(1, h)
        attend(2, h)
        hop_one(h).start()
        forward(2, h).start()
        return carry

    lax.fori_loop(0, heads, inner, 0)

    def outer(h, carry):
        for copy in halo_copies(h):
            copy.wait_recv()
        attend(0, h)
        attend(3, h)
        forward(0, h).start()
        forward(3, h).start()
        hop_one(h).wait_recv()
        hop_two(h).start()
        return carry

    lax.fori_loop(0, heads, outer, 0)

    def last(h, carry):
        hop_two(h).wait_recv()
        hop_three(h).start()
        for copy in halo_copies(h):
            copy.wait_send()
        return carry

    lax.fori_loop(0, heads, last, 0)

    def whole(ref, send, recv):
        return pltpu.make_async_remote_copy(
            src_ref=ref,
            dst_ref=ref,
            send_sem=send,
            recv_sem=recv,
            device_id=(ahead, p, t),
            device_id_type=MESH,
        )

    whole(stage, out_send, out_recv).wait_send()
    whole(relay_one, one_send, out_recv).wait_send()
    whole(relay_two, two_send, out_recv).wait_send()
    whole(out_ref, out_send, out_recv).wait_recv()


def per_device(sections, homes, queries, keys, values, seg_len):
    _, rows, feats = queries.shape
    heads = feats // HEAD_DIM
    segs = seg_len.shape[2]
    blocks = rows // BLOCK
    bf16 = jnp.bfloat16
    dma = pltpu.SemaphoreType.DMA
    handed = pl.pallas_call(
        functools.partial(kernel, (sections, homes, heads, rows, segs)),
        out_shape=jax.ShapeDtypeStruct((rows // 2, 2 * feats), bf16),
        in_specs=[pl.BlockSpec(memory_space=pltpu.SMEM)] + [pl.BlockSpec(memory_space=pl.ANY)] * 3,
        out_specs=pl.BlockSpec(memory_space=pl.ANY),
        scratch_shapes=[
            pltpu.VMEM((rows, feats), bf16),
            pltpu.VMEM((rows + 2 * HALO, feats), bf16),
            pltpu.VMEM((rows + 2 * HALO, feats), bf16),
            pltpu.VMEM((blocks, BLOCK, WINDOW), jnp.float32),
            pltpu.VMEM((blocks, heads, BLOCK, HEAD_DIM), bf16),
            pltpu.VMEM((heads, BLOCK, HEAD_DIM), bf16),
            pltpu.VMEM((heads, BLOCK, HEAD_DIM), bf16),
            dma((3,)),
            dma((4, heads)),
            dma((4, heads)),
            dma,
            dma,
            dma((heads,)),
            dma,
            dma((heads,)),
            dma,
        ],
        compiler_params=pltpu.CompilerParams(
            collective_id=0, has_side_effects=True, vmem_limit_bytes=56 * 1024 * 1024
        ),
        cost_estimate=pl.CostEstimate(
            flops=4 * rows * WINDOW * feats,
            bytes_accessed=8 * rows * feats,
            transcendentals=rows * WINDOW * heads,
        ),
        name="segment_attention",
    )(jnp.swapaxes(seg_len, 1, 2), queries, keys, values)
    return handed[None]


def solution(mesh):
    sections, homes = mesh.shape["section"], mesh.shape["pack"]
    return jax.shard_map(
        functools.partial(per_device, sections, homes),
        mesh=mesh,
        in_specs=(
            P("section", "pack", "tensor"),
            P("section", "pack", "tensor"),
            P("section", "pack", "tensor"),
            P(),
        ),
        out_specs=P("section", ("pack", "tensor"), None),
        check_vma=False,
    )
```

```python
import functools
import math

import jax
import jax.numpy as jnp
from jax import lax
from jax.experimental import pallas as pl
from jax.experimental.pallas import tpu as pltpu
from jax.sharding import PartitionSpec as P

HEAD_DIM = 128
HALO = 64
BLOCK = 128
WINDOW = BLOCK + 2 * HALO
MESH = pl.DeviceIdType.MESH
MASKED = -3.0e38
GROUP = 2


def kernel(
    sizes,
    len_hbm,
    q_hbm,
    k_hbm,
    v_hbm,
    out_ref,
    q_buf,
    k_buf,
    v_buf,
    bias,
    stage,
    relay_one,
    relay_two,
    len_ref,
    len_sem,
    load_sem,
    halo_send,
    halo_recv,
    out_send,
    out_recv,
    one_recv,
    one_send,
    two_recv,
    two_send,
):
    sections, homes, heads, rows, segs = sizes
    feats = heads * HEAD_DIM
    s, p, t = lax.axis_index("section"), lax.axis_index("pack"), lax.axis_index("tensor")
    ahead, behind = lax.rem(s + 1, sections), lax.rem(s + sections - 1, sections)
    after, before = lax.rem(p + 1, homes), lax.rem(p + homes - 1, homes)

    barrier = pltpu.get_barrier_semaphore()
    has_after, has_before = p < homes - 1, p > 0

    def greet(partner):
        pl.semaphore_signal(barrier, inc=1, device_id=partner, device_id_type=MESH)

    partners = [(ahead, p, t), (ahead, p, 1 - t), (behind, p, t), (behind, p, 1 - t)]
    for partner in partners:
        greet(partner)

    @pl.when(has_after)
    def _():
        greet((s, after, t))

    @pl.when(has_before)
    def _():
        greet((s, before, t))

    fetch_lengths = pltpu.make_async_copy(len_hbm.at[s], len_ref, len_sem)
    fetch_lengths.start()

    units = heads // GROUP
    width = GROUP * HEAD_DIM

    def unit_cols(u):
        return pl.ds(pl.multiple_of(u * width, width), width)

    def loads(u):
        cols, own = unit_cols(u), pl.ds(HALO, rows)
        return [
            pltpu.make_async_copy(q_hbm.at[0, :, cols], q_buf.at[:, cols], load_sem.at[0, u]),
            pltpu.make_async_copy(k_hbm.at[0, :, cols], k_buf.at[own, cols], load_sem.at[1, u]),
            pltpu.make_async_copy(v_hbm.at[0, :, cols], v_buf.at[own, cols], load_sem.at[2, u]),
        ]

    def start_loads(u, carry):
        for load in loads(u):
            load.start()
        return carry

    lax.fori_loop(0, units, start_loads, 0)

    @pl.when(jnp.logical_not(has_before))
    def _():
        k_buf[0:HALO] = jnp.zeros((HALO, feats), jnp.bfloat16)
        v_buf[0:HALO] = jnp.zeros((HALO, feats), jnp.bfloat16)

    @pl.when(jnp.logical_not(has_after))
    def _():
        k_buf[HALO + rows :] = jnp.zeros((HALO, feats), jnp.bfloat16)
        v_buf[HALO + rows :] = jnp.zeros((HALO, feats), jnp.bfloat16)

    fetch_lengths.wait()

    thresholds = [jnp.where(has_before, -len_ref[segs - 1, before], 0)]
    end = jnp.int32(0)
    for j in range(segs - 1):
        end = end + len_ref[j, p]
        thresholds.append(end)
    thresholds.append(rows + jnp.where(has_after, len_ref[0, after], 0))

    def labels(position):
        total = jnp.zeros(position.shape, jnp.int32)
        for threshold in thresholds:
            total = total + jnp.where(position >= threshold, 1, 0)
        return total

    key_label = labels(lax.broadcasted_iota(jnp.int32, (8, rows + 2 * HALO), 1) - HALO)
    for b in range(rows // BLOCK):
        query_label = labels(lax.broadcasted_iota(jnp.int32, (BLOCK, 128), 0) + b * BLOCK)
        for c in range(WINDOW // 128):
            start = b * BLOCK + c * 128
            same = query_label == key_label[0:1, start : start + 128]
            bias[b, :, c * 128 : c * 128 + 128] = jnp.where(same, 0.0, MASKED)

    def halo(u, side):
        cols = unit_cols(u)
        low, high = pl.ds(0, HALO), pl.ds(rows - HALO, HALO)
        source_rows, target_rows, home = (
            (high, pl.ds(0, HALO), after) if side == 0 else (low, pl.ds(HALO + rows, HALO), before)
        )
        return [
            pltpu.make_async_remote_copy(
                src_ref=source.at[0, source_rows, cols],
                dst_ref=buf.at[target_rows, cols],
                send_sem=halo_send.at[2 * side + n, u],
                recv_sem=halo_recv.at[2 * side + n, u],
                device_id=(s, home, t),
                device_id_type=MESH,
            )
            for n, (source, buf) in enumerate(((k_hbm, k_buf), (v_hbm, v_buf)))
        ]

    def each_side(act, conditions):
        for side, condition in enumerate(conditions):

            @pl.when(condition)
            def _():
                act(side)

    factor = math.log2(math.e) / math.sqrt(HEAD_DIM)

    def attend(b, u):
        for g in range(GROUP):
            cols = pl.ds(pl.multiple_of(u * width, width) + g * HEAD_DIM, HEAD_DIM)
            scores = lax.dot_general(
                q_buf[b * BLOCK : (b + 1) * BLOCK, cols],
                k_buf[b * BLOCK : b * BLOCK + WINDOW, cols],
                (((1,), (1,)), ((), ())),
                preferred_element_type=jnp.float32,
            )
            scores = scores + bias[b]
            row_max = jnp.max(scores, axis=1, keepdims=True)
            weights = jnp.exp2((scores - row_max) * factor)
            weights = weights * (1.0 / jnp.sum(weights, axis=1, keepdims=True))
            mixed = jnp.dot(
                weights.astype(jnp.bfloat16),
                v_buf[b * BLOCK : b * BLOCK + WINDOW, cols],
                preferred_element_type=jnp.float32,
            )
            stage[b, u, :, g * HEAD_DIM : (g + 1) * HEAD_DIM] = mixed.astype(jnp.bfloat16)

    def final_place(b, u):
        start = pl.multiple_of(t * feats + u * width, HEAD_DIM)
        return out_ref.at[pl.ds((b % 2) * BLOCK, BLOCK), pl.ds(start, width)]

    def forward(b, u):
        return pltpu.make_async_remote_copy(
            src_ref=stage.at[b, u],
            dst_ref=final_place(b, u),
            send_sem=out_send,
            recv_sem=out_recv,
            device_id=(ahead, p, b // 2),
            device_id_type=MESH,
        )

    def hop_one(u):
        return pltpu.make_async_remote_copy(
            src_ref=stage.at[1, u],
            dst_ref=relay_one.at[u],
            send_sem=out_send,
            recv_sem=one_recv.at[u],
            device_id=(behind, p, t),
            device_id_type=MESH,
        )

    def hop_two(u):
        return pltpu.make_async_remote_copy(
            src_ref=relay_one.at[u],
            dst_ref=relay_two.at[u],
            send_sem=one_send,
            recv_sem=two_recv.at[u],
            device_id=(behind, p, t),
            device_id_type=MESH,
        )

    def hop_three(u):
        return pltpu.make_async_remote_copy(
            src_ref=relay_two.at[u],
            dst_ref=final_place(1, u),
            send_sem=two_send,
            recv_sem=out_recv,
            device_id=(behind, p, 0),
            device_id_type=MESH,
        )

    def make_inner(u):
        for load in loads(u):
            load.wait()
        attend(1, u)
        attend(2, u)

    def send_inner(u):
        hop_one(u).start()
        forward(2, u).start()
        each_side(lambda side: [copy.start() for copy in halo(u, side)], (has_after, has_before))

    make_inner(0)

    pack_peers = jnp.where(has_after, 1, 0) + jnp.where(has_before, 1, 0)
    pl.semaphore_wait(barrier, len(partners) + pack_peers)

    def inner(u, carry):
        send_inner(u - 1)
        make_inner(u)
        return carry

    lax.fori_loop(1, units, inner, 0)
    send_inner(units - 1)

    def outer(u, carry):
        each_side(lambda side: [copy.wait_recv() for copy in halo(u, side)], (has_before, has_after))
        attend(0, u)
        attend(3, u)
        forward(0, u).start()
        forward(3, u).start()
        hop_one(u).wait_recv()
        hop_two(u).start()
        return carry

    lax.fori_loop(0, units, outer, 0)

    def last(u, carry):
        hop_two(u).wait_recv()
        hop_three(u).start()
        each_side(lambda side: [copy.wait_send() for copy in halo(u, side)], (has_after, has_before))
        return carry

    lax.fori_loop(0, units, last, 0)

    def whole(ref, send, recv):
        return pltpu.make_async_remote_copy(
            src_ref=ref,
            dst_ref=ref,
            send_sem=send,
            recv_sem=recv,
            device_id=(ahead, p, t),
            device_id_type=MESH,
        )

    whole(stage, out_send, out_recv).wait_send()
    whole(relay_one, one_send, out_recv).wait_send()
    whole(relay_two, two_send, out_recv).wait_send()
    whole(out_ref, out_send, out_recv).wait_recv()


def per_device(sections, homes, queries, keys, values, seg_len):
    _, rows, feats = queries.shape
    heads = feats // HEAD_DIM
    segs = seg_len.shape[2]
    blocks, units, width = rows // BLOCK, heads // GROUP, GROUP * HEAD_DIM
    bf16 = jnp.bfloat16
    dma = pltpu.SemaphoreType.DMA
    handed = pl.pallas_call(
        functools.partial(kernel, (sections, homes, heads, rows, segs)),
        out_shape=jax.ShapeDtypeStruct((rows // 2, 2 * feats), bf16),
        in_specs=[pl.BlockSpec(memory_space=pl.ANY)] * 4,
        out_specs=pl.BlockSpec(memory_space=pl.ANY),
        scratch_shapes=[
            pltpu.VMEM((rows, feats), bf16),
            pltpu.VMEM((rows + 2 * HALO, feats), bf16),
            pltpu.VMEM((rows + 2 * HALO, feats), bf16),
            pltpu.VMEM((blocks, BLOCK, WINDOW), jnp.float32),
            pltpu.VMEM((blocks, units, BLOCK, width), bf16),
            pltpu.VMEM((units, BLOCK, width), bf16),
            pltpu.VMEM((units, BLOCK, width), bf16),
            pltpu.SMEM((segs, homes), jnp.int32),
            dma,
            dma((3, units)),
            dma((4, units)),
            dma((4, units)),
            dma,
            dma,
            dma((units,)),
            dma,
            dma((units,)),
            dma,
        ],
        compiler_params=pltpu.CompilerParams(
            collective_id=0, has_side_effects=True, vmem_limit_bytes=12 * 1024 * 1024
        ),
        cost_estimate=pl.CostEstimate(
            flops=4 * rows * WINDOW * feats,
            bytes_accessed=8 * rows * feats,
            transcendentals=rows * WINDOW * heads,
        ),
        name="segment_attention",
    )(*(pltpu.with_memory_space_constraint(x, pltpu.HBM) for x in (jnp.swapaxes(seg_len, 1, 2), queries, keys, values)))
    return handed[None]


def solution(mesh):
    sections, homes = mesh.shape["section"], mesh.shape["pack"]
    return jax.shard_map(
        functools.partial(per_device, sections, homes),
        mesh=mesh,
        in_specs=(
            P("section", "pack", "tensor"),
            P("section", "pack", "tensor"),
            P("section", "pack", "tensor"),
            P(),
        ),
        out_specs=P("section", ("pack", "tensor"), None),
        check_vma=False,
    )
```

```python
import functools
import math

import jax
import jax.numpy as jnp
from jax import lax
from jax.experimental import pallas as pl
from jax.experimental.pallas import tpu as pltpu
from jax.sharding import PartitionSpec as P

HEAD_DIM = 128
HALO = 64
BLOCK = 128
WINDOW = BLOCK + 2 * HALO
MESH = pl.DeviceIdType.MESH
MASKED = -3.0e38
GROUP = 2
ROW = 4


def kernel(
    sizes,
    len_hbm,
    q_hbm,
    k_hbm,
    v_hbm,
    out_ref,
    q_buf,
    k_buf,
    v_buf,
    bias,
    stage,
    relay_one,
    relay_two,
    extra,
    extra_recv,
    extra_send,
    ready,
    len_ref,
    len_sem,
    load_sem,
    halo_send,
    halo_recv,
    out_send,
    out_recv,
    one_recv,
    one_send,
    two_recv,
    two_send,
):
    sections, homes, heads, rows, segs = sizes
    feats = heads * HEAD_DIM
    s, p, t = lax.axis_index("section"), lax.axis_index("pack"), lax.axis_index("tensor")
    ahead, behind = lax.rem(s + 1, sections), lax.rem(s + sections - 1, sections)
    after, before = lax.rem(p + 1, homes), lax.rem(p + homes - 1, homes)

    has_after, has_before = p < homes - 1, p > 0

    barrier = pltpu.get_barrier_semaphore()

    def greet(partner):
        pl.semaphore_signal(barrier, inc=1, device_id=partner, device_id_type=MESH)

    partners = [(ahead, p, t), (ahead, p, 1 - t), (behind, p, t), (behind, p, 1 - t)]
    for partner in partners:
        greet(partner)

    far_after = (p >= homes // 2) & (lax.rem(p, ROW) == ROW - 1) & has_after
    far_before = (p > homes // 2) & (lax.rem(p, ROW) == 0)

    @pl.when(has_after & jnp.logical_not(far_after))
    def _():
        greet((s, after, t))

    @pl.when(has_before)
    def _():
        greet((s, before, t))

    fetch_lengths = pltpu.make_async_copy(len_hbm.at[s], len_ref, len_sem)
    fetch_lengths.start()

    units = heads // GROUP
    width = GROUP * HEAD_DIM

    def unit_cols(u):
        return pl.ds(pl.multiple_of(u * width, width), width)

    def loads(u):
        cols, own = unit_cols(u), pl.ds(HALO, rows)
        return [
            pltpu.make_async_copy(q_hbm.at[0, :, cols], q_buf.at[:, cols], load_sem.at[0, u]),
            pltpu.make_async_copy(k_hbm.at[0, :, cols], k_buf.at[own, cols], load_sem.at[1, u]),
            pltpu.make_async_copy(v_hbm.at[0, :, cols], v_buf.at[own, cols], load_sem.at[2, u]),
        ]

    def start_loads(u, carry):
        for load in loads(u):
            load.start()
        return carry

    lax.fori_loop(0, units, start_loads, 0)

    @pl.when(jnp.logical_not(has_before))
    def _():
        k_buf[0:HALO] = jnp.zeros((HALO, feats), jnp.bfloat16)
        v_buf[0:HALO] = jnp.zeros((HALO, feats), jnp.bfloat16)

    @pl.when(jnp.logical_not(has_after))
    def _():
        k_buf[HALO + rows :] = jnp.zeros((HALO, feats), jnp.bfloat16)
        v_buf[HALO + rows :] = jnp.zeros((HALO, feats), jnp.bfloat16)

    fetch_lengths.wait()

    thresholds = [jnp.where(has_before, -len_ref[segs - 1, before], 0)]
    end = jnp.int32(0)
    for j in range(segs - 1):
        end = end + len_ref[j, p]
        thresholds.append(end)
    thresholds.append(rows + jnp.where(has_after, len_ref[0, after], 0))

    def labels(position):
        total = jnp.zeros(position.shape, jnp.int32)
        for threshold in thresholds:
            total = total + jnp.where(position >= threshold, 1, 0)
        return total

    key_label = labels(lax.broadcasted_iota(jnp.int32, (8, rows + 2 * HALO), 1) - HALO)
    for b in range(rows // BLOCK):
        query_label = labels(lax.broadcasted_iota(jnp.int32, (BLOCK, 128), 0) + b * BLOCK)
        for c in range(WINDOW // 128):
            start = b * BLOCK + c * 128
            same = query_label == key_label[0:1, start : start + 128]
            bias[b, :, c * 128 : c * 128 + 128] = jnp.where(same, 0.0, MASKED)

    def halo(u, side):
        cols = unit_cols(u)
        low, high = pl.ds(0, HALO), pl.ds(rows - HALO, HALO)
        source_rows, target_rows, home = (
            (high, pl.ds(0, HALO), after) if side == 0 else (low, pl.ds(HALO + rows, HALO), before)
        )
        return [
            pltpu.make_async_remote_copy(
                src_ref=source.at[0, source_rows, cols],
                dst_ref=buf.at[target_rows, cols],
                send_sem=halo_send.at[2 * side + n, u],
                recv_sem=halo_recv.at[2 * side + n, u],
                device_id=(s, home, t),
                device_id_type=MESH,
            )
            for n, (source, buf) in enumerate(((k_hbm, k_buf), (v_hbm, v_buf)))
        ]

    def each_side(act, conditions):
        for side, condition in enumerate(conditions):

            @pl.when(condition)
            def _():
                act(side)

    factor = math.log2(math.e) / math.sqrt(HEAD_DIM)

    def attend(b, h):
        cols = pl.ds(pl.multiple_of(h * HEAD_DIM, HEAD_DIM), HEAD_DIM)
        scores = lax.dot_general(
            q_buf[b * BLOCK : (b + 1) * BLOCK, cols],
            k_buf[b * BLOCK : b * BLOCK + WINDOW, cols],
            (((1,), (1,)), ((), ())),
            preferred_element_type=jnp.float32,
        )
        scores = scores + bias[b]
        row_max = jnp.max(scores, axis=1, keepdims=True)
        weights = jnp.exp2((scores - row_max) * factor)
        weights = weights * (1.0 / jnp.sum(weights, axis=1, keepdims=True))
        mixed = jnp.dot(
            weights.astype(jnp.bfloat16),
            v_buf[b * BLOCK : b * BLOCK + WINDOW, cols],
            preferred_element_type=jnp.float32,
        )
        stage[b, :, cols] = mixed.astype(jnp.bfloat16)

    def final_place(b, u):
        start = pl.multiple_of(t * feats + u * width, HEAD_DIM)
        return out_ref.at[pl.ds((b % 2) * BLOCK, BLOCK), pl.ds(start, width)]

    def copy_to(source, target, send, recv, device):
        return pltpu.make_async_remote_copy(
            src_ref=source,
            dst_ref=target,
            send_sem=send,
            recv_sem=recv,
            device_id=device,
            device_id_type=MESH,
        )

    def forward(b, u):
        source = stage.at[b, :, unit_cols(u)]
        return copy_to(source, final_place(b, u), out_send, out_recv, (ahead, p, b // 2))

    def hop_one(u):
        cols = unit_cols(u)
        return copy_to(stage.at[1, :, cols], relay_one.at[:, cols], out_send, one_recv.at[u], (behind, p, t))

    def hop_two(u):
        cols = unit_cols(u)
        return copy_to(relay_one.at[:, cols], relay_two.at[:, cols], one_send, two_recv.at[u], (behind, p, t))

    def hop_three(u):
        source = relay_two.at[:, unit_cols(u)]
        return copy_to(source, final_place(1, u), two_send, out_recv, (behind, p, 0))

    def make(u, blocks):
        for g in range(GROUP):
            for b in blocks:
                attend(b, u * GROUP + g)

    def make_inner(u):
        for load in loads(u):
            load.wait()
        make(u, (1, 2))

    def send_inner(u):
        hop_one(u).start()
        forward(2, u).start()

    def start_halos(conditions):
        def start_halo(u, carry):
            each_side(lambda side: [copy.start() for copy in halo(u, side)], conditions)
            return carry

        lax.fori_loop(0, units, start_halo, 0)

    make_inner(0)

    pack_peers = jnp.where(has_after, 1, 0) + jnp.where(has_before & jnp.logical_not(far_before), 1, 0)
    pl.semaphore_wait(barrier, len(partners) + pack_peers)

    @pl.when(far_after)
    def _():
        pl.semaphore_signal(ready, inc=1, device_id=(s, after, t), device_id_type=MESH)

    send_inner(0)
    start_halos((has_after, has_before & jnp.logical_not(far_before)))

    def inner(u, carry):
        make_inner(u)
        send_inner(u)
        return carry

    lax.fori_loop(1, units - 1, inner, 0)

    end_cols = pl.ds(feats - HEAD_DIM, HEAD_DIM)
    extra_one = copy_to(stage.at[2, :, end_cols], extra.at[0], out_send, extra_recv.at[0], (behind, p, t))
    extra_two = copy_to(extra.at[0], extra.at[1], extra_send.at[0], extra_recv.at[1], (behind, p, t))
    extra_start = pl.multiple_of(t * feats + feats - HEAD_DIM, HEAD_DIM)
    extra_place = out_ref.at[pl.ds(0, BLOCK), pl.ds(extra_start, HEAD_DIM)]
    extra_three = copy_to(extra.at[1], extra_place, extra_send.at[1], out_recv, (behind, p, 1))
    is_last = s == sections - 1

    make_inner(units - 1)
    hop_one(units - 1).start()

    @pl.when(jnp.logical_not(is_last))
    def _():
        forward(2, units - 1).start()

    @pl.when(is_last)
    def _():
        part_start = (units - 1) * width
        part_place = out_ref.at[
            pl.ds(0, BLOCK), pl.ds(pl.multiple_of(t * feats + part_start, HEAD_DIM), width - HEAD_DIM)
        ]
        part = stage.at[2, :, pl.ds(part_start, width - HEAD_DIM)]
        extra_one.start()
        copy_to(part, part_place, out_send, out_recv, (ahead, p, 1)).start()

    @pl.when(far_before)
    def _():
        pl.semaphore_wait(ready, 1)

        def start_before(u, carry):
            for copy in halo(u, 1):
                copy.start()
            return carry

        lax.fori_loop(0, units, start_before, 0)

    def outer(b, relays):
        side, exists = (0, has_before) if b == 0 else (1, has_after)

        def step(u, carry):
            @pl.when(exists)
            def _():
                for copy in halo(u, side):
                    copy.wait_recv()

            make(u, (b,))
            forward(b, u).start()
            if relays:
                hop_one(u).wait_recv()
                hop_two(u).start()
            return carry

        lax.fori_loop(0, units, step, 0)

    def both_outer(first, second):
        outer(first, True)

        @pl.when(s == sections - 2)
        def _():
            extra_one.wait_recv()
            extra_two.start()

        outer(second, False)

    row_end = lax.rem(p, ROW) == ROW - 1

    @pl.when(jnp.logical_not(row_end))
    def _():
        both_outer(3, 0)

    @pl.when(row_end)
    def _():
        both_outer(0, 3)

    def last(u, carry):
        hop_two(u).wait_recv()
        hop_three(u).start()
        return carry

    lax.fori_loop(0, units - 2, last, 0)

    @pl.when(s == sections - 3)
    def _():
        extra_two.wait_recv()
        extra_three.start()

    lax.fori_loop(units - 2, units, last, 0)

    @pl.when(s == sections - 3)
    def _():
        extra_three.wait_send()

    @pl.when(s == sections - 2)
    def _():
        extra_two.wait_send()

    def end_halo(u, carry):
        each_side(lambda side: [copy.wait_send() for copy in halo(u, side)], (has_after, has_before))
        return carry

    lax.fori_loop(0, units, end_halo, 0)

    def whole(ref, send, recv):
        return pltpu.make_async_remote_copy(
            src_ref=ref,
            dst_ref=ref,
            send_sem=send,
            recv_sem=recv,
            device_id=(ahead, p, t),
            device_id_type=MESH,
        )

    whole(out_ref, out_send, out_recv).wait_send()
    whole(relay_one, one_send, out_recv).wait_send()
    whole(relay_two, two_send, out_recv).wait_send()
    whole(out_ref, out_send, out_recv).wait_recv()


def per_device(sections, homes, queries, keys, values, seg_len):
    _, rows, feats = queries.shape
    heads = feats // HEAD_DIM
    segs = seg_len.shape[2]
    blocks, units = rows // BLOCK, heads // GROUP
    bf16 = jnp.bfloat16
    dma = pltpu.SemaphoreType.DMA
    handed = pl.pallas_call(
        functools.partial(kernel, (sections, homes, heads, rows, segs)),
        out_shape=jax.ShapeDtypeStruct((rows // 2, 2 * feats), bf16),
        in_specs=[pl.BlockSpec(memory_space=pl.ANY)] * 4,
        out_specs=pl.BlockSpec(memory_space=pl.ANY),
        scratch_shapes=[
            pltpu.VMEM((rows, feats), bf16),
            pltpu.VMEM((rows + 2 * HALO, feats), bf16),
            pltpu.VMEM((rows + 2 * HALO, feats), bf16),
            pltpu.VMEM((blocks, BLOCK, WINDOW), jnp.float32),
            pltpu.VMEM((blocks, BLOCK, feats), bf16),
            pltpu.VMEM((BLOCK, feats), bf16),
            pltpu.VMEM((BLOCK, feats), bf16),
            pltpu.VMEM((2, BLOCK, HEAD_DIM), bf16),
            dma((2,)),
            dma((2,)),
            pltpu.SemaphoreType.REGULAR,
            pltpu.SMEM((segs, homes), jnp.int32),
            dma,
            dma((3, units)),
            dma((4, units)),
            dma((4, units)),
            dma,
            dma,
            dma((units,)),
            dma,
            dma((units,)),
            dma,
        ],
        compiler_params=pltpu.CompilerParams(
            collective_id=0, has_side_effects=True, vmem_limit_bytes=12 * 1024 * 1024
        ),
        cost_estimate=pl.CostEstimate(
            flops=4 * rows * WINDOW * feats,
            bytes_accessed=8 * rows * feats,
            transcendentals=rows * WINDOW * heads,
        ),
        name="segment_attention",
    )(*(pltpu.with_memory_space_constraint(x, pltpu.HBM) for x in (jnp.swapaxes(seg_len, 1, 2), queries, keys, values)))
    return handed[None]


def solution(mesh):
    sections, homes = mesh.shape["section"], mesh.shape["pack"]
    return jax.shard_map(
        functools.partial(per_device, sections, homes),
        mesh=mesh,
        in_specs=(
            P("section", "pack", "tensor"),
            P("section", "pack", "tensor"),
            P("section", "pack", "tensor"),
            P(),
        ),
        out_specs=P("section", ("pack", "tensor"), None),
        check_vma=False,
    )
```

```python
import functools
import math

import jax
import jax.numpy as jnp
from jax import lax
from jax.experimental import pallas as pl
from jax.experimental.pallas import tpu as pltpu
from jax.sharding import PartitionSpec as P

HEAD_DIM = 128
HALO = 64
BLOCK = 128
WINDOW = BLOCK + 2 * HALO
MESH = pl.DeviceIdType.MESH
MASKED = -3.0e38
GROUP = 2
ROW = 4


def kernel(
    sizes,
    len_hbm,
    q_hbm,
    k_hbm,
    v_hbm,
    out_ref,
    q_buf,
    k_buf,
    v_buf,
    bias,
    stage,
    relay_one,
    relay_two,
    extra,
    extra_recv,
    extra_send,
    ready,
    len_ref,
    len_sem,
    load_sem,
    halo_send,
    halo_recv,
    out_send,
    out_recv,
    one_recv,
    one_send,
    two_recv,
    two_send,
):
    sections, homes, heads, rows, segs = sizes
    feats = heads * HEAD_DIM
    s, p, t = lax.axis_index("section"), lax.axis_index("pack"), lax.axis_index("tensor")
    ahead, behind = lax.rem(s + 1, sections), lax.rem(s + sections - 1, sections)
    after, before = lax.rem(p + 1, homes), lax.rem(p + homes - 1, homes)

    has_after, has_before = p < homes - 1, p > 0

    barrier = pltpu.get_barrier_semaphore()

    def greet(partner):
        pl.semaphore_signal(barrier, inc=1, device_id=partner, device_id_type=MESH)

    partners = [(ahead, p, t), (ahead, p, 1 - t), (behind, p, t), (behind, p, 1 - t)]
    for partner in partners:
        greet(partner)

    mid_after, mid_before = p == homes // 2 - 1, p == homes // 2
    far_after = (lax.rem(p, ROW) == ROW - 1) & has_after & jnp.logical_not(mid_after)
    far_before = (lax.rem(p, ROW) == 0) & has_before & jnp.logical_not(mid_before)
    near_after = has_after & jnp.logical_not(mid_after)
    near_before = has_before & jnp.logical_not(far_before)

    @pl.when(has_after & jnp.logical_not(far_after))
    def _():
        greet((s, after, t))

    @pl.when(has_before & jnp.logical_not(mid_before))
    def _():
        greet((s, before, t))

    units = heads // GROUP
    width = GROUP * HEAD_DIM

    def unit_cols(u):
        return pl.ds(pl.multiple_of(u * width, width), width)

    def loads(u):
        cols, own = unit_cols(u), pl.ds(HALO, rows)
        return [
            pltpu.make_async_copy(q_hbm.at[0, :, cols], q_buf.at[:, cols], load_sem.at[0, u]),
            pltpu.make_async_copy(k_hbm.at[0, :, cols], k_buf.at[own, cols], load_sem.at[1, u]),
            pltpu.make_async_copy(v_hbm.at[0, :, cols], v_buf.at[own, cols], load_sem.at[2, u]),
        ]

    def start_loads(u, carry):
        for load in loads(u):
            load.start()
        return carry

    fetch_lengths = pltpu.make_async_copy(len_hbm.at[s], len_ref, len_sem)
    start_loads(0, 0)
    fetch_lengths.start()

    @pl.when(jnp.logical_not(has_before))
    def _():
        k_buf[0:HALO] = jnp.zeros((HALO, feats), jnp.bfloat16)
        v_buf[0:HALO] = jnp.zeros((HALO, feats), jnp.bfloat16)

    @pl.when(jnp.logical_not(has_after))
    def _():
        k_buf[HALO + rows :] = jnp.zeros((HALO, feats), jnp.bfloat16)
        v_buf[HALO + rows :] = jnp.zeros((HALO, feats), jnp.bfloat16)

    fetch_lengths.wait()

    thresholds = [jnp.where(has_before, -len_ref[segs - 1, before], 0)]
    end = jnp.int32(0)
    for j in range(segs - 1):
        end = end + len_ref[j, p]
        thresholds.append(end)
    thresholds.append(rows + jnp.where(has_after, len_ref[0, after], 0))

    def labels(position):
        total = jnp.zeros(position.shape, jnp.int32)
        for threshold in thresholds:
            total = total + jnp.where(position >= threshold, 1, 0)
        return total

    key_label = labels(lax.broadcasted_iota(jnp.int32, (8, rows + 2 * HALO), 1) - HALO)
    def make_bias(b):
        query_label = labels(lax.broadcasted_iota(jnp.int32, (BLOCK, 128), 0) + b * BLOCK)
        for c in range(WINDOW // 128):
            start = b * BLOCK + c * 128
            same = query_label == key_label[0:1, start : start + 128]
            bias[b, :, c * 128 : c * 128 + 128] = jnp.where(same, 0.0, MASKED)

    make_bias(1)
    make_bias(2)

    def halo(u, side):
        cols = unit_cols(u)
        low, high = pl.ds(0, HALO), pl.ds(rows - HALO, HALO)
        source_rows, target_rows, home = (
            (high, pl.ds(0, HALO), after) if side == 0 else (low, pl.ds(HALO + rows, HALO), before)
        )
        return [
            pltpu.make_async_remote_copy(
                src_ref=source.at[0, source_rows, cols],
                dst_ref=buf.at[target_rows, cols],
                send_sem=halo_send.at[2 * side + n, u],
                recv_sem=halo_recv.at[2 * side + n, u],
                device_id=(s, home, t),
                device_id_type=MESH,
            )
            for n, (source, buf) in enumerate(((k_hbm, k_buf), (v_hbm, v_buf)))
        ]

    def each_side(act, conditions):
        for side, condition in enumerate(conditions):

            @pl.when(condition)
            def _():
                act(side)

    factor = math.log2(math.e) / math.sqrt(HEAD_DIM)

    def final_place(b, u):
        start = pl.multiple_of(t * feats + u * width, HEAD_DIM)
        return out_ref.at[pl.ds((b % 2) * BLOCK, BLOCK), pl.ds(start, width)]

    def copy_to(source, target, send, recv, device):
        return pltpu.make_async_remote_copy(
            src_ref=source,
            dst_ref=target,
            send_sem=send,
            recv_sem=recv,
            device_id=device,
            device_id_type=MESH,
        )

    def forward(b, u):
        source = stage.at[b, :, unit_cols(u)]
        return copy_to(source, final_place(b, u), out_send, out_recv, (ahead, p, b // 2))

    def hop_one(u):
        cols = unit_cols(u)
        return copy_to(stage.at[1, :, cols], relay_one.at[:, cols], out_send, one_recv.at[u], (behind, p, t))

    def hop_two(u):
        cols = unit_cols(u)
        return copy_to(relay_one.at[:, cols], relay_two.at[:, cols], one_send, two_recv.at[u], (behind, p, t))

    def hop_three(u):
        source = relay_two.at[:, unit_cols(u)]
        return copy_to(source, final_place(1, u), two_send, out_recv, (behind, p, 0))

    def make(u, blocks):
        places = [
            (b, pl.ds(pl.multiple_of(u * width, width) + g * HEAD_DIM, HEAD_DIM))
            for g in range(GROUP)
            for b in blocks
        ]
        scores = [
            lax.dot_general(
                q_buf[b * BLOCK : (b + 1) * BLOCK, cols],
                k_buf[b * BLOCK : b * BLOCK + WINDOW, cols],
                (((1,), (1,)), ((), ())),
                preferred_element_type=jnp.float32,
            )
            + bias[b]
            for b, cols in places
        ]
        maxima = [jnp.max(score, axis=1, keepdims=True) for score in scores]
        weights = [jnp.exp2((score - top) * factor) for score, top in zip(scores, maxima)]
        sums = [jnp.sum(weight, axis=1, keepdims=True) for weight in weights]
        weights = [(weight * (1.0 / total)).astype(jnp.bfloat16) for weight, total in zip(weights, sums)]
        mixed = [
            jnp.dot(weight, v_buf[b * BLOCK : b * BLOCK + WINDOW, cols], preferred_element_type=jnp.float32)
            for weight, (b, cols) in zip(weights, places)
        ]
        for value, (b, cols) in zip(mixed, places):
            stage[b, :, cols] = value.astype(jnp.bfloat16)

    def make_inner(u):
        for load in loads(u):
            load.wait()
        make(u, (1, 2))

    def send_inner(u):
        hop_one(u).start()
        forward(2, u).start()

    def start_halos(conditions):
        def start_halo(u, carry):
            each_side(lambda side: [copy.start() for copy in halo(u, side)], conditions)
            return carry

        lax.fori_loop(0, units, start_halo, 0)

    for load in loads(0):
        load.wait()
    lax.fori_loop(1, units, start_loads, 0)
    make(0, (1, 2))

    pack_peers = jnp.where(near_after, 1, 0) + jnp.where(near_before, 1, 0)
    pl.semaphore_wait(barrier, len(partners) + pack_peers)

    @pl.when(far_after)
    def _():
        pl.semaphore_signal(ready, inc=1, device_id=(s, after, t), device_id_type=MESH)

    @pl.when(mid_before)
    def _():
        pl.semaphore_signal(ready, inc=1, device_id=(s, before, t), device_id_type=MESH)

    send_inner(0)
    start_halos((near_after, near_before))

    def inner(u, carry):
        make_inner(u)
        send_inner(u)
        return carry

    lax.fori_loop(1, units - 1, inner, 0)

    end_cols = pl.ds(feats - HEAD_DIM, HEAD_DIM)
    extra_one = copy_to(stage.at[2, :, end_cols], extra.at[0], out_send, extra_recv.at[0], (behind, p, t))
    extra_two = copy_to(extra.at[0], extra.at[1], extra_send.at[0], extra_recv.at[1], (behind, p, t))
    extra_start = pl.multiple_of(t * feats + feats - HEAD_DIM, HEAD_DIM)
    extra_place = out_ref.at[pl.ds(0, BLOCK), pl.ds(extra_start, HEAD_DIM)]
    extra_three = copy_to(extra.at[1], extra_place, extra_send.at[1], out_recv, (behind, p, 1))
    is_last = s == sections - 1

    make_inner(units - 1)
    hop_one(units - 1).start()

    @pl.when(jnp.logical_not(is_last))
    def _():
        forward(2, units - 1).start()

    @pl.when(is_last)
    def _():
        part_start = (units - 1) * width
        part_place = out_ref.at[
            pl.ds(0, BLOCK), pl.ds(pl.multiple_of(t * feats + part_start, HEAD_DIM), width - HEAD_DIM)
        ]
        part = stage.at[2, :, pl.ds(part_start, width - HEAD_DIM)]
        extra_one.start()
        copy_to(part, part_place, out_send, out_recv, (ahead, p, 1)).start()

    make_bias(0)
    make_bias(3)

    @pl.when(far_before | mid_after)
    def _():
        pl.semaphore_wait(ready, 1)
        start_halos((mid_after, far_before))

    def outer(b, relays):
        side, exists = (0, has_before) if b == 0 else (1, has_after)

        def step(u, carry):
            @pl.when(exists)
            def _():
                for copy in halo(u, side):
                    copy.wait_recv()

            make(u, (b,))
            if relays:
                forward(b, u).start()
                hop_one(u).wait_recv()
                hop_two(u).start()
            return carry

        if relays:
            lax.fori_loop(0, units, step, 0)
        else:
            for first, end in ((0, 2), (2, units)):
                lax.fori_loop(first, end, step, 0)
                cols = pl.ds(first * width, (end - first) * width)
                start = pl.multiple_of(t * feats + first * width, HEAD_DIM)
                place = out_ref.at[
                    pl.ds((b % 2) * BLOCK, BLOCK), pl.ds(start, (end - first) * width)
                ]
                copy_to(stage.at[b, :, cols], place, out_send, out_recv, (ahead, p, b // 2)).start()

    def both_outer(first, second):
        outer(first, True)

        @pl.when(s == sections - 2)
        def _():
            extra_one.wait_recv()
            extra_two.start()

        outer(second, False)

    row_end = lax.rem(p, ROW) == ROW - 1

    @pl.when(jnp.logical_not(row_end))
    def _():
        both_outer(3, 0)

    @pl.when(row_end)
    def _():
        both_outer(0, 3)

    def last(u, carry):
        hop_two(u).wait_recv()
        hop_three(u).start()
        return carry

    lax.fori_loop(0, units - 2, last, 0)

    @pl.when(s == sections - 3)
    def _():
        extra_two.wait_recv()
        extra_three.start()

    lax.fori_loop(units - 2, units, last, 0)

    @pl.when(s == sections - 3)
    def _():
        extra_three.wait_send()

    @pl.when(s == sections - 2)
    def _():
        extra_two.wait_send()

    def end_halo(u, carry):
        each_side(lambda side: [copy.wait_send() for copy in halo(u, side)], (has_after, has_before))
        return carry

    lax.fori_loop(0, units, end_halo, 0)

    def whole(ref, send, recv):
        return pltpu.make_async_remote_copy(
            src_ref=ref,
            dst_ref=ref,
            send_sem=send,
            recv_sem=recv,
            device_id=(ahead, p, t),
            device_id_type=MESH,
        )

    whole(out_ref, out_send, out_recv).wait_send()
    whole(relay_one, one_send, out_recv).wait_send()
    whole(relay_two, two_send, out_recv).wait_send()
    whole(out_ref, out_send, out_recv).wait_recv()


def per_device(sections, homes, queries, keys, values, seg_len):
    _, rows, feats = queries.shape
    heads = feats // HEAD_DIM
    segs = seg_len.shape[2]
    blocks, units = rows // BLOCK, heads // GROUP
    bf16 = jnp.bfloat16
    dma = pltpu.SemaphoreType.DMA
    handed = pl.pallas_call(
        functools.partial(kernel, (sections, homes, heads, rows, segs)),
        out_shape=jax.ShapeDtypeStruct((rows // 2, 2 * feats), bf16),
        in_specs=[pl.BlockSpec(memory_space=pl.ANY)] * 4,
        out_specs=pl.BlockSpec(memory_space=pl.ANY),
        scratch_shapes=[
            pltpu.VMEM((rows, feats), bf16),
            pltpu.VMEM((rows + 2 * HALO, feats), bf16),
            pltpu.VMEM((rows + 2 * HALO, feats), bf16),
            pltpu.VMEM((blocks, BLOCK, WINDOW), jnp.float32),
            pltpu.VMEM((blocks, BLOCK, feats), bf16),
            pltpu.VMEM((BLOCK, feats), bf16),
            pltpu.VMEM((BLOCK, feats), bf16),
            pltpu.VMEM((2, BLOCK, HEAD_DIM), bf16),
            dma((2,)),
            dma((2,)),
            pltpu.SemaphoreType.REGULAR,
            pltpu.SMEM((segs, homes), jnp.int32),
            dma,
            dma((3, units)),
            dma((4, units)),
            dma((4, units)),
            dma,
            dma,
            dma((units,)),
            dma,
            dma((units,)),
            dma,
        ],
        compiler_params=pltpu.CompilerParams(
            collective_id=0, has_side_effects=True, vmem_limit_bytes=12 * 1024 * 1024
        ),
        cost_estimate=pl.CostEstimate(
            flops=4 * rows * WINDOW * feats,
            bytes_accessed=8 * rows * feats,
            transcendentals=rows * WINDOW * heads,
        ),
        name="segment_attention",
    )(*(pltpu.with_memory_space_constraint(x, pltpu.HBM) for x in (jnp.swapaxes(seg_len, 1, 2), queries, keys, values)))
    return handed[None]


def solution(mesh):
    sections, homes = mesh.shape["section"], mesh.shape["pack"]
    return jax.shard_map(
        functools.partial(per_device, sections, homes),
        mesh=mesh,
        in_specs=(
            P("section", "pack", "tensor"),
            P("section", "pack", "tensor"),
            P("section", "pack", "tensor"),
            P(),
        ),
        out_specs=P("section", ("pack", "tensor"), None),
        check_vma=False,
    )
```

```python
import functools
import math

import jax
import jax.numpy as jnp
from jax import lax
from jax.experimental import pallas as pl
from jax.experimental.pallas import tpu as pltpu
from jax.sharding import PartitionSpec as P

HEAD_DIM = 128
HALO = 64
BLOCK = 128
WINDOW = BLOCK + 2 * HALO
MESH = pl.DeviceIdType.MESH
MASKED = -3.0e38
GROUP = 2
ROW = 4


def kernel(
    sizes,
    len_hbm,
    q_hbm,
    k_hbm,
    v_hbm,
    out_ref,
    q_buf,
    k_buf,
    v_buf,
    bias,
    stage,
    relay_one,
    relay_two,
    extra,
    extra_recv,
    extra_send,
    ready,
    len_ref,
    len_sem,
    load_sem,
    halo_send,
    halo_recv,
    out_send,
    out_recv,
    one_recv,
    one_send,
    two_recv,
    two_send,
):
    sections, homes, heads, rows, segs = sizes
    feats = heads * HEAD_DIM
    s, p, t = lax.axis_index("section"), lax.axis_index("pack"), lax.axis_index("tensor")
    ahead, behind = lax.rem(s + 1, sections), lax.rem(s + sections - 1, sections)
    after, before = lax.rem(p + 1, homes), lax.rem(p + homes - 1, homes)

    has_after, has_before = p < homes - 1, p > 0

    barrier = pltpu.get_barrier_semaphore()

    def greet(partner):
        pl.semaphore_signal(barrier, inc=1, device_id=partner, device_id_type=MESH)

    partners = [(ahead, p, t), (ahead, p, 1 - t), (behind, p, t), (behind, p, 1 - t)]
    for partner in partners:
        greet(partner)

    mid_after, mid_before = p == homes // 2 - 1, p == homes // 2
    far_after = (lax.rem(p, ROW) == ROW - 1) & has_after & jnp.logical_not(mid_after)
    far_before = (lax.rem(p, ROW) == 0) & has_before & jnp.logical_not(mid_before)
    near_after = has_after & jnp.logical_not(mid_after)
    near_before = has_before & jnp.logical_not(far_before)

    @pl.when(has_after & jnp.logical_not(far_after))
    def _():
        greet((s, after, t))

    @pl.when(has_before & jnp.logical_not(mid_before))
    def _():
        greet((s, before, t))

    units = heads // GROUP
    width = GROUP * HEAD_DIM

    def unit_cols(u):
        return pl.ds(pl.multiple_of(u * width, width), width)

    def loads(u):
        cols, own = unit_cols(u), pl.ds(HALO, rows)
        return [
            pltpu.make_async_copy(q_hbm.at[0, :, cols], q_buf.at[:, cols], load_sem.at[0, u]),
            pltpu.make_async_copy(k_hbm.at[0, :, cols], k_buf.at[own, cols], load_sem.at[1, u]),
            pltpu.make_async_copy(v_hbm.at[0, :, cols], v_buf.at[own, cols], load_sem.at[2, u]),
        ]

    def start_loads(u, carry):
        for load in loads(u):
            load.start()
        return carry

    fetch_lengths = pltpu.make_async_copy(len_hbm.at[s], len_ref, len_sem)
    start_loads(0, 0)
    fetch_lengths.start()

    @pl.when(jnp.logical_not(has_before))
    def _():
        k_buf[0:HALO] = jnp.zeros((HALO, feats), jnp.bfloat16)
        v_buf[0:HALO] = jnp.zeros((HALO, feats), jnp.bfloat16)

    @pl.when(jnp.logical_not(has_after))
    def _():
        k_buf[HALO + rows :] = jnp.zeros((HALO, feats), jnp.bfloat16)
        v_buf[HALO + rows :] = jnp.zeros((HALO, feats), jnp.bfloat16)

    fetch_lengths.wait()

    thresholds = [jnp.where(has_before, -len_ref[segs - 1, before], 0)]
    end = jnp.int32(0)
    for j in range(segs - 1):
        end = end + len_ref[j, p]
        thresholds.append(end)
    thresholds.append(rows + jnp.where(has_after, len_ref[0, after], 0))

    def labels(position):
        total = jnp.zeros(position.shape, jnp.int32)
        for threshold in thresholds:
            total = total + jnp.where(position >= threshold, 1, 0)
        return total

    key_label = labels(lax.broadcasted_iota(jnp.int32, (8, rows + 2 * HALO), 1) - HALO)
    def make_bias(b):
        query_label = labels(lax.broadcasted_iota(jnp.int32, (BLOCK, 128), 0) + b * BLOCK)
        for c in range(WINDOW // 128):
            start = b * BLOCK + c * 128
            same = query_label == key_label[0:1, start : start + 128]
            bias[b, :, c * 128 : c * 128 + 128] = jnp.where(same, 0.0, MASKED)

    make_bias(1)
    make_bias(2)

    def halo(u, side):
        cols = unit_cols(u)
        low, high = pl.ds(0, HALO), pl.ds(rows - HALO, HALO)
        source_rows, target_rows, home = (
            (high, pl.ds(0, HALO), after) if side == 0 else (low, pl.ds(HALO + rows, HALO), before)
        )
        return [
            pltpu.make_async_remote_copy(
                src_ref=source.at[0, source_rows, cols],
                dst_ref=buf.at[target_rows, cols],
                send_sem=halo_send.at[2 * side + n, u],
                recv_sem=halo_recv.at[2 * side + n, u],
                device_id=(s, home, t),
                device_id_type=MESH,
            )
            for n, (source, buf) in enumerate(((k_hbm, k_buf), (v_hbm, v_buf)))
        ]

    def each_side(act, conditions):
        for side, condition in enumerate(conditions):

            @pl.when(condition)
            def _():
                act(side)

    factor = math.log2(math.e) / math.sqrt(HEAD_DIM)

    def final_place(b, u):
        start = pl.multiple_of(t * feats + u * width, HEAD_DIM)
        return out_ref.at[pl.ds((b % 2) * BLOCK, BLOCK), pl.ds(start, width)]

    def copy_to(source, target, send, recv, device):
        return pltpu.make_async_remote_copy(
            src_ref=source,
            dst_ref=target,
            send_sem=send,
            recv_sem=recv,
            device_id=device,
            device_id_type=MESH,
        )

    def forward(b, u):
        source = stage.at[b, :, unit_cols(u)]
        return copy_to(source, final_place(b, u), out_send, out_recv, (ahead, p, b // 2))

    def forward_heads(b, first, count):
        cols = pl.ds(pl.multiple_of(first * HEAD_DIM, HEAD_DIM), count * HEAD_DIM)
        start = pl.multiple_of(t * feats + first * HEAD_DIM, HEAD_DIM)
        place = out_ref.at[pl.ds((b % 2) * BLOCK, BLOCK), pl.ds(start, count * HEAD_DIM)]
        return copy_to(stage.at[b, :, cols], place, out_send, out_recv, (ahead, p, b // 2))

    def hop_one(u):
        cols = unit_cols(u)
        return copy_to(stage.at[1, :, cols], relay_one.at[:, cols], out_send, one_recv.at[u], (behind, p, t))

    def hop_two(u):
        cols = unit_cols(u)
        return copy_to(relay_one.at[:, cols], relay_two.at[:, cols], one_send, two_recv.at[u], (behind, p, t))

    def hop_three(u):
        source = relay_two.at[:, unit_cols(u)]
        return copy_to(source, final_place(1, u), two_send, out_recv, (behind, p, 0))

    def make(u, blocks):
        places = [
            (b, pl.ds(pl.multiple_of(u * width, width) + g * HEAD_DIM, HEAD_DIM))
            for g in range(GROUP)
            for b in blocks
        ]
        scores = [
            lax.dot_general(
                q_buf[b * BLOCK : (b + 1) * BLOCK, cols],
                k_buf[b * BLOCK : b * BLOCK + WINDOW, cols],
                (((1,), (1,)), ((), ())),
                preferred_element_type=jnp.float32,
            )
            + bias[b]
            for b, cols in places
        ]
        maxima = [jnp.max(score, axis=1, keepdims=True) for score in scores]
        weights = [jnp.exp2((score - top) * factor) for score, top in zip(scores, maxima)]
        sums = [jnp.sum(weight, axis=1, keepdims=True) for weight in weights]
        weights = [(weight * (1.0 / total)).astype(jnp.bfloat16) for weight, total in zip(weights, sums)]
        mixed = [
            jnp.dot(weight, v_buf[b * BLOCK : b * BLOCK + WINDOW, cols], preferred_element_type=jnp.float32)
            for weight, (b, cols) in zip(weights, places)
        ]
        for value, (b, cols) in zip(mixed, places):
            stage[b, :, cols] = value.astype(jnp.bfloat16)

    def make_inner(u):
        for load in loads(u):
            load.wait()
        make(u, (1, 2))

    def send_inner(u):
        hop_one(u).start()
        forward(2, u).start()

    def start_halos(conditions):
        def start_halo(u, carry):
            each_side(lambda side: [copy.start() for copy in halo(u, side)], conditions)
            return carry

        lax.fori_loop(0, units, start_halo, 0)

    for load in loads(0):
        load.wait()
    lax.fori_loop(1, units, start_loads, 0)
    make(0, (1, 2))

    pack_peers = jnp.where(near_after, 1, 0) + jnp.where(near_before, 1, 0)
    pl.semaphore_wait(barrier, len(partners) + pack_peers)

    @pl.when(far_after)
    def _():
        pl.semaphore_signal(ready, inc=1, device_id=(s, after, t), device_id_type=MESH)

    @pl.when(mid_before)
    def _():
        pl.semaphore_signal(ready, inc=1, device_id=(s, before, t), device_id_type=MESH)

    send_inner(0)
    start_halos((near_after, near_before))

    def inner(u, carry):
        make_inner(u)
        send_inner(u)
        return carry

    lax.fori_loop(1, units - 1, inner, 0)

    end_cols = pl.ds(feats - HEAD_DIM, HEAD_DIM)
    extra_one = copy_to(stage.at[2, :, end_cols], extra.at[0], out_send, extra_recv.at[0], (behind, p, t))
    extra_two = copy_to(extra.at[0], extra.at[1], extra_send.at[0], extra_recv.at[1], (behind, p, t))
    extra_start = pl.multiple_of(t * feats + feats - HEAD_DIM, HEAD_DIM)
    extra_place = out_ref.at[pl.ds(0, BLOCK), pl.ds(extra_start, HEAD_DIM)]
    extra_three = copy_to(extra.at[1], extra_place, extra_send.at[1], out_recv, (behind, p, 1))
    is_last = s == sections - 1

    make_inner(units - 1)
    hop_one(units - 1).start()

    @pl.when(jnp.logical_not(is_last))
    def _():
        forward(2, units - 1).start()

    @pl.when(is_last)
    def _():
        part_start = (units - 1) * width
        part_place = out_ref.at[
            pl.ds(0, BLOCK), pl.ds(pl.multiple_of(t * feats + part_start, HEAD_DIM), width - HEAD_DIM)
        ]
        part = stage.at[2, :, pl.ds(part_start, width - HEAD_DIM)]
        extra_one.start()
        copy_to(part, part_place, out_send, out_recv, (ahead, p, 1)).start()

    make_bias(0)
    make_bias(3)

    @pl.when(far_before | mid_after)
    def _():
        pl.semaphore_wait(ready, 1)
        start_halos((mid_after, far_before))

    def outer(b, relays):
        side, exists = (0, has_before) if b == 0 else (1, has_after)

        def step(u, carry):
            @pl.when(exists)
            def _():
                for copy in halo(u, side):
                    copy.wait_recv()

            make(u, (b,))
            if relays:

                @pl.when(lax.rem(u, 2) == 1)
                def _():
                    forward_heads(b, (u - 1) * GROUP, 2 * GROUP).start()

                @pl.when(u == units - 1)
                def _():
                    forward(b, u).start()

                hop_one(u).wait_recv()
                hop_two(u).start()
            return carry

        if relays:
            lax.fori_loop(0, units, step, 0)
        else:
            first = 0
            for end in (units,):
                lax.fori_loop(first, end, step, 0)
                forward_heads(b, first * GROUP, (end - first) * GROUP).start()
                first = end

    def both_outer(first, second):
        outer(first, True)

        @pl.when(s == sections - 2)
        def _():
            extra_one.wait_recv()
            extra_two.start()

        outer(second, False)

    row_end = lax.rem(p, ROW) == ROW - 1

    @pl.when(jnp.logical_not(row_end))
    def _():
        both_outer(3, 0)

    @pl.when(row_end)
    def _():
        both_outer(0, 3)

    def last(u, carry):
        hop_two(u).wait_recv()
        hop_three(u).start()
        return carry

    lax.fori_loop(0, units - 2, last, 0)

    @pl.when(s == sections - 3)
    def _():
        extra_two.wait_recv()
        extra_three.start()

    lax.fori_loop(units - 2, units, last, 0)

    @pl.when(s == sections - 3)
    def _():
        extra_three.wait_send()

    @pl.when(s == sections - 2)
    def _():
        extra_two.wait_send()

    def end_halo(u, carry):
        each_side(lambda side: [copy.wait_send() for copy in halo(u, side)], (has_after, has_before))
        return carry

    lax.fori_loop(0, units, end_halo, 0)

    def whole(ref, send, recv):
        return pltpu.make_async_remote_copy(
            src_ref=ref,
            dst_ref=ref,
            send_sem=send,
            recv_sem=recv,
            device_id=(ahead, p, t),
            device_id_type=MESH,
        )

    whole(out_ref, out_send, out_recv).wait_send()
    whole(relay_one, one_send, out_recv).wait_send()
    whole(relay_two, two_send, out_recv).wait_send()
    whole(out_ref, out_send, out_recv).wait_recv()


def per_device(sections, homes, queries, keys, values, seg_len):
    _, rows, feats = queries.shape
    heads = feats // HEAD_DIM
    segs = seg_len.shape[2]
    blocks, units = rows // BLOCK, heads // GROUP
    bf16 = jnp.bfloat16
    dma = pltpu.SemaphoreType.DMA
    handed = pl.pallas_call(
        functools.partial(kernel, (sections, homes, heads, rows, segs)),
        out_shape=jax.ShapeDtypeStruct((rows // 2, 2 * feats), bf16),
        in_specs=[pl.BlockSpec(memory_space=pl.ANY)] * 4,
        out_specs=pl.BlockSpec(memory_space=pl.ANY),
        scratch_shapes=[
            pltpu.VMEM((rows, feats), bf16),
            pltpu.VMEM((rows + 2 * HALO, feats), bf16),
            pltpu.VMEM((rows + 2 * HALO, feats), bf16),
            pltpu.VMEM((blocks, BLOCK, WINDOW), jnp.float32),
            pltpu.VMEM((blocks, BLOCK, feats), bf16),
            pltpu.VMEM((BLOCK, feats), bf16),
            pltpu.VMEM((BLOCK, feats), bf16),
            pltpu.VMEM((2, BLOCK, HEAD_DIM), bf16),
            dma((2,)),
            dma((2,)),
            pltpu.SemaphoreType.REGULAR,
            pltpu.SMEM((segs, homes), jnp.int32),
            dma,
            dma((3, units)),
            dma((4, units)),
            dma((4, units)),
            dma,
            dma,
            dma((units,)),
            dma,
            dma((units,)),
            dma,
        ],
        compiler_params=pltpu.CompilerParams(
            collective_id=0, has_side_effects=True, vmem_limit_bytes=12 * 1024 * 1024
        ),
        cost_estimate=pl.CostEstimate(
            flops=4 * rows * WINDOW * feats,
            bytes_accessed=8 * rows * feats,
            transcendentals=rows * WINDOW * heads,
        ),
        name="segment_attention",
    )(*(pltpu.with_memory_space_constraint(x, pltpu.HBM) for x in (jnp.swapaxes(seg_len, 1, 2), queries, keys, values)))
    return handed[None]


def solution(mesh):
    sections, homes = mesh.shape["section"], mesh.shape["pack"]
    return jax.shard_map(
        functools.partial(per_device, sections, homes),
        mesh=mesh,
        in_specs=(
            P("section", "pack", "tensor"),
            P("section", "pack", "tensor"),
            P("section", "pack", "tensor"),
            P(),
        ),
        out_specs=P("section", ("pack", "tensor"), None),
        check_vma=False,
    )
```
